32 devices in a mesh: corpus: 8 (over z, y), query: 4 (over x, core).
Axes of the slice: x: 2, y: 2, z: 4, core: 2. Of those that a mesh axis runs over, the one named last changes fastest.
Arguments:
- queries: bfloat16 [8192, 768], P(('corpus', 'query')), may hold values from -8 to 8
- probes: int32 [8192, 4], P(('corpus', 'query')), may hold values from 0 to 255, as said below
- targets: int32 [8192, 8], P(('corpus', 'query')), may hold values from 0 to 4095, all different within a row
- passage_codes: int32 [256, 96, 1024], P('corpus'), may hold values from 0 to 15
- codebook: float32 [16, 768], replicated, may hold values from -6 to 6
Outputs:
- grad_queries: bfloat16 [8192, 768], P(('corpus', 'query'))
- codebook_step: float32 [16, 768], replicated
The draws below stay inside these ranges and needn't reach their ends.
Inputs may be any that keep to these rules, and one draw needn't show every extreme that they name: `probes`: each row names 4 different lists; list l belongs to index l // 32 of corpus. In every aligned block of 256 rows (the rows of one device) no list is named more than 8 times, and one list, the same one in every block, is named exactly 8 times. `targets`: each row names 8 different candidates; column r holds the candidate of rank r.
All inputs are finite; a program needn't handle non-finite values.
Results may differ from the reference program's by a relative error of at most 0.01.
The reference program's roundings to bfloat16 on the way count: a program that leaves them out, or rounds other values in their place, can miss the bound.
Values may be sent and summed in bfloat16 or wider, within the bound.
A program may use at most 192 MiB of HBM per device.

```python
import math
import jax
import jax.numpy as jnp
import numpy as np
from jax import lax

D = 768
SUBSPACES = 96
CENTROIDS = 16
SUBDIM = 8
PASSAGES = 1024
PROBES = 4
TARGETS = 8
Q_DEV = 256
LISTS = 256
CAP = 8
QUERIES = 8192


def draw_queries(key, part):
    column_key = jax.random.fold_in(key, 11)
    spread = jnp.exp(jax.random.uniform(column_key, (D,), jnp.float32, jnp.log(0.01), jnp.log(0.1)))
    values = jax.random.truncated_normal(jax.random.fold_in(key, 17), -6.0, 6.0, (QUERIES, D), jnp.float32) * spread[None, :]
    return jnp.clip(values, -8.0, 8.0).astype(jnp.bfloat16)


def draw_probes(key, part):
    blocks = QUERIES // Q_DEV
    others = LISTS - 1
    hot_list = jax.random.randint(jax.random.fold_in(key, 21), (), 0, LISTS)

    def block_probes(block_key):
        sub_keys = jax.random.split(block_key, 4)
        list_cycle = jax.random.permutation(sub_keys[0], others).astype(jnp.int32)
        list_cycle = list_cycle + (list_cycle >= hot_list).astype(jnp.int32)
        offset = jax.random.randint(sub_keys[1], (), 0, others)
        row_order = jax.random.permutation(sub_keys[2], Q_DEV).astype(jnp.int32)
        row_rank = jnp.zeros((Q_DEV,), jnp.int32).at[row_order].set(jnp.arange(Q_DEV, dtype=jnp.int32))
        is_hot = row_rank < CAP
        first_entry = jnp.where(is_hot, (PROBES - 1) * row_rank, (PROBES - 1) * CAP + PROBES * (row_rank - CAP))
        probe_cols = jnp.arange(PROBES, dtype=jnp.int32)
        entry_index = first_entry[:, None] + jnp.where(is_hot[:, None], probe_cols[None, :] - 1, probe_cols[None, :])
        chosen = list_cycle[(entry_index + offset) % others]
        base_lists = jnp.where(is_hot[:, None] & (probe_cols == 0)[None, :], hot_list, chosen)
        rotation = jax.random.randint(sub_keys[3], (Q_DEV, 1), 0, PROBES)
        column_index = (probe_cols[None, :] - rotation) % PROBES
        return jnp.take_along_axis(base_lists, column_index, axis=1)
    block_keys = jax.random.split(jax.random.fold_in(key, 22), blocks)
    return jax.vmap(block_probes)(block_keys).reshape(QUERIES, PROBES).astype(jnp.int32)


def place_ends(drawn, rng, least, high):
    extent = drawn.shape
    index_at = [jax.random.randint(jax.random.fold_in(rng, axis), (), 0, extent[axis]) for axis in range(len(extent))]
    drawn = drawn.at[tuple(index_at)].set(least)
    longest = extent.index(max(extent))
    index_at[longest] = (index_at[longest] + 1) % extent[longest]
    return drawn.at[tuple(index_at)].set(high)


def cumulative_ranks(amount, lean):
    weights = [(1 << 20) // math.isqrt(grade ** lean) + 1 for grade in range(1, amount + 1)]
    scale = 1 + sum(weights) // (1 << 30)
    return np.cumsum(np.array([max(1, weight // scale) for weight in weights]))


def skewed_ids(own_key, shape, number_of, lean):
    listing = cumulative_ranks(number_of, lean)
    ticket = jax.random.randint(jax.random.fold_in(own_key, 1), shape, 0, int(listing[number_of - 1]))
    rank = jnp.searchsorted(jnp.asarray(listing, jnp.int32), ticket, side="right")
    return jax.random.permutation(jax.random.fold_in(own_key, 2), number_of)[rank].astype(jnp.int32)


def choose_distinct(stream_key, rows, count, top, lift):
    sequence = jax.random.permutation(jax.random.fold_in(stream_key, 1), count)
    favour = sequence
    for power in range(3):
        favour = favour * favour // count
    favour = favour * lift // count
    lots = jax.random.randint(jax.random.fold_in(stream_key, 2), (rows, count), 0, 4096) + favour
    fixed_rows = jax.random.permutation(jax.random.fold_in(stream_key, 3), rows)[jnp.arange(count) % rows]
    lots = jnp.where(jnp.arange(rows)[:, None] == fixed_rows[None, :], 1 << 14, lots)
    score = lots * count + jnp.arange(count)
    return lax.top_k(score.astype(jnp.int32), top)[1].astype(jnp.int32)


def bell_draw(key, dims, scale, bound, held_as=jnp.bfloat16):
    return jnp.clip(scale * jax.random.normal(key, dims, jnp.float32), -bound, bound).astype(held_as)


def setup_inputs(seed: int = 0) -> dict:
    keys = jax.random.split(jax.random.key(seed), 6)
    queries = draw_queries(jax.random.fold_in(keys[5], 71), 0)
    probes = draw_probes(jax.random.fold_in(keys[5], 71), 0)
    targets = choose_distinct(keys[2], QUERIES, PROBES * PASSAGES, TARGETS, 0)
    passage_codes = place_ends(skewed_ids(keys[3], (LISTS, SUBSPACES, PASSAGES), CENTROIDS, 2), jax.random.fold_in(keys[3], 3), 0, CENTROIDS - 1).astype(jnp.int32)
    codebook = bell_draw(keys[4], (CENTROIDS, D), 1.0, 6.0, jnp.float32)
    return dict(queries=queries, probes=probes, targets=targets, passage_codes=passage_codes, codebook=codebook)


EPSILON = 1e-06
NEGATIVE = -1e+30

def rank_weights():
    levels = jnp.arange(TARGETS).astype(jnp.int32).astype(jnp.float32)
    return 2.0 * (TARGETS - levels) / (TARGETS * (TARGETS + 1.0))

def centroid_table(code_list):
    levels = jnp.arange(CENTROIDS).astype(jnp.int32)
    marked = code_list[:, None, :] == levels[None, :, None]
    return marked.astype(jnp.float32).reshape(SUBSPACES * CENTROIDS, PASSAGES)

def reference(queries, probes, targets, passage_codes, codebook):
    highest = lax.Precision.HIGHEST
    blocks = QUERIES // Q_DEV
    per_block = Q_DEV * PROBES
    entries = QUERIES * PROBES
    column_cap = blocks * CAP
    centroids = codebook.reshape(CENTROIDS, SUBSPACES, SUBDIM)
    split_queries = queries.astype(jnp.float32).reshape(QUERIES, SUBSPACES, SUBDIM)
    lookup = jnp.einsum('qme,kme->qmk', split_queries, centroids, precision=highest)
    lookup = lookup.reshape(QUERIES, SUBSPACES * CENTROIDS).astype(jnp.bfloat16)
    list_ids = jnp.arange(LISTS).astype(jnp.int32)

    def block_ranks(block_probes):
        marked = (block_probes[:, None] == list_ids[None, :]).astype(jnp.int32)
        running = jnp.cumsum(marked, axis=0)
        return lax.optimization_barrier(jnp.sum(marked * running, axis=1)) - 1
    flat_probes = probes.reshape(blocks, per_block)
    block_rank = lax.map(block_ranks, flat_probes)
    block_index = jnp.arange(blocks).astype(jnp.int32)[:, None]
    position = (flat_probes * column_cap + block_index * CAP + block_rank).reshape(entries)
    entry_at = jnp.full((LISTS * column_cap,), -1, jnp.int32).at[position].set(jnp.arange(entries).astype(jnp.int32))
    probe_cols = jnp.arange(PROBES).astype(jnp.int32)
    inside = targets[:, None, :] // PASSAGES == probe_cols[None, :, None]
    target_spot = jnp.where(inside, targets[:, None, :] % PASSAGES, -1).reshape(entries, TARGETS)
    weights = rank_weights()
    places = jnp.arange(PASSAGES).astype(jnp.int32)

    def list_scores(list_index):
        owned_ids = lax.dynamic_slice_in_dim(entry_at, list_index * column_cap, column_cap)
        is_valid = owned_ids >= 0
        safe_id = jnp.maximum(owned_ids, 0)
        lut_rows = lookup[safe_id // PROBES].astype(jnp.float32)
        one_hot = centroid_table(passage_codes[list_index])
        scores = jnp.dot(lut_rows, one_hot, precision=highest)
        return (is_valid, safe_id, scores, one_hot)

    def first_pass(list_index):
        is_valid, safe_id, scores, one_hot = list_scores(list_index)
        top_score = lax.optimization_barrier(jnp.max(scores, axis=1))
        exp_total = lax.optimization_barrier(jnp.sum(jnp.exp(scores - top_score[:, None]), axis=1))
        return (jnp.where(is_valid, top_score, NEGATIVE), jnp.where(is_valid, exp_total, 0.0))
    slot_top, slot_total = lax.map(first_pass, jnp.arange(LISTS).astype(jnp.int32))
    entry_top = slot_top.reshape(-1)[position].reshape(QUERIES, PROBES)
    entry_total = slot_total.reshape(-1)[position].reshape(QUERIES, PROBES)
    query_top = lax.optimization_barrier(jnp.max(entry_top, axis=1))
    query_total = lax.optimization_barrier(jnp.sum(entry_total * jnp.exp(entry_top - query_top[:, None]), axis=1))

    def second_pass(state_pair, list_index):
        grad_sum, book_sum = state_pair
        is_valid, safe_id, scores, one_hot = list_scores(list_index)
        owner_query = safe_id // PROBES
        spots = target_spot[safe_id]
        teacher = lax.optimization_barrier(jnp.sum(jnp.where(spots[:, :, None] == places[None, None, :], weights[None, :, None], 0.0), axis=1))
        student = jnp.exp(scores - query_top[owner_query][:, None]) / query_total[owner_query][:, None]
        grad_scores = jnp.where(is_valid[:, None], student - teacher, 0.0).astype(jnp.bfloat16)
        histogram = jnp.dot(grad_scores.astype(jnp.float32), one_hot.T, precision=highest)
        histogram = histogram.reshape(column_cap, SUBSPACES, CENTROIDS)
        partial_value = jnp.einsum('rmk,kme->rme', histogram, centroids, precision=highest).reshape(column_cap, D)
        grad_sum = grad_sum.at[owner_query].add(jnp.where(is_valid[:, None], partial_value, 0.0))
        chosen_rows = split_queries[owner_query]
        book_sum = book_sum + jnp.einsum('rmk,rme->kme', histogram, chosen_rows, precision=highest)
        return ((grad_sum, book_sum), None)
    initial = (jnp.zeros((QUERIES, D), jnp.float32), jnp.zeros((CENTROIDS, SUBSPACES, SUBDIM), jnp.float32))
    (grad_sum, book_sum), ignored = lax.scan(second_pass, initial, jnp.arange(LISTS).astype(jnp.int32))
    raw_grad = book_sum.reshape(CENTROIDS, D)
    normed = raw_grad * lax.rsqrt(jnp.mean(raw_grad * raw_grad) + EPSILON)
    return (grad_sum.astype(jnp.bfloat16), normed)
```

```python
import functools

import jax
import jax.numpy as jnp
from jax import lax
from jax.experimental import pallas as pl
from jax.experimental.pallas import tpu as pltpu
from jax.sharding import PartitionSpec as P

D = 768
SUBSPACES = 96
CENTROIDS = 16
SUBDIM = 8
PASSAGES = 1024
PROBES = 4
TARGETS = 8
EPSILON = 1e-06

CHUNK = 128
CHUNKS = D // CHUNK
SPACES = CHUNK // SUBDIM
COLS = SPACES * CENTROIDS
NOTES = 128
WIDE = D + NOTES

NT = (((1,), (1,)), ((), ()))
TN = (((0,), (0,)), ((), ()))


def dot(a, b, dims=(((1,), (0,)), ((), ()))):
    return lax.dot_general(a, b, dims, preferred_element_type=jnp.float32)


def split(x, parts):
    out = []
    for _ in range(parts):
        top = x.astype(jnp.bfloat16)
        out.append(top)
        x = x - top.astype(jnp.float32)
    return out


def diagonal(shape):
    row = lax.broadcasted_iota(jnp.int32, shape, 1)
    col = lax.broadcasted_iota(jnp.int32, shape, 2)
    return row == col // SUBDIM


def fill_table(cb_ref, table):
    for c in range(CHUNKS):
        cb = cb_ref[:, c * CHUNK : (c + 1) * CHUNK]
        spread = jnp.broadcast_to(cb[:, None, :], (CENTROIDS, SPACES, CHUNK))
        spread = jnp.where(diagonal(spread.shape), spread, 0.0).reshape(COLS, CHUNK)
        for i, part in enumerate(split(spread, 3)):
            table[i, c] = part


def one_hot(codes_ref, c):
    codes = codes_ref[0, c * SPACES : (c + 1) * SPACES, :]
    return jnp.concatenate(
        [jnp.where(codes == k, 1.0, 0.0).astype(jnp.bfloat16) for k in range(CENTROIDS)], axis=0
    )


def score_kernel(off_ref, rows_ref, codes_ref, cb_ref, exp_ref, stat_ref, table):
    @pl.when(pl.program_id(0) == 0)
    def _():
        fill_table(cb_ref, table)

    scores = None
    for c in range(CHUNKS):
        row = rows_ref[0, :, c * CHUNK : (c + 1) * CHUNK]
        lut = dot(row, table[2, c], NT) + dot(row, table[1, c], NT) + dot(row, table[0, c], NT)
        term = dot(lut.astype(jnp.bfloat16), one_hot(codes_ref, c))
        scores = term if scores is None else scores + term
    top = jnp.max(scores, axis=1, keepdims=True)
    e = jnp.exp(scores - top)
    exp_ref[0] = e
    total = jnp.sum(e, axis=1, keepdims=True)
    lane = lax.broadcasted_iota(jnp.int32, (e.shape[0], 128), 1)
    stat_ref[0] = jnp.where(lane == 0, top, total).T[:8]


def grad_kernel(
    off_ref, rows_ref, codes_ref, cb_ref, exp_ref, factor_ref, part_ref, raw_ref, table, raw
):
    step = pl.program_id(0)

    @pl.when(step == 0)
    def _():
        fill_table(cb_ref, table)
        raw[...] = jnp.zeros_like(raw)

    slots = exp_ref.shape[1]
    factor = jnp.broadcast_to(factor_ref[0], (128, slots)).T[:, 0:1]
    notes = rows_ref[0, :, D:].astype(jnp.float32)
    place = lax.broadcasted_iota(jnp.int32, (slots, PASSAGES), 1)
    teacher = jnp.zeros((slots, PASSAGES), jnp.float32)
    for r in range(TARGETS):
        spot = (notes[:, r : r + 1] - 1.0) * 256.0 + notes[:, TARGETS + r : TARGETS + r + 1]
        weight = 2.0 * (TARGETS - r) / (TARGETS * (TARGETS + 1.0))
        teacher = jnp.where(place == spot.astype(jnp.int32), weight, teacher)
    grad = (exp_ref[0] * factor - teacher).astype(jnp.bfloat16)
    for c in range(CHUNKS):
        hist = dot(grad, one_hot(codes_ref, c), NT)
        hi, lo = split(hist, 2)
        part = dot(hi, table[0, c]) + dot(hi, table[1, c]) + dot(lo, table[0, c])
        part_ref[0, :, c * CHUNK : (c + 1) * CHUNK] = part.astype(jnp.bfloat16)
        row = rows_ref[0, :, c * CHUNK : (c + 1) * CHUNK]
        raw[c] += dot(hi, row, TN) + dot(lo, row, TN)

    @pl.when(step == pl.num_programs(0) - 1)
    def _():
        for c in range(CHUNKS):
            grid = raw[c].reshape(CENTROIDS, SPACES, CHUNK)
            kept = jnp.where(diagonal(grid.shape), grid, 0.0)
            raw_ref[:, c * CHUNK : (c + 1) * CHUNK] = jnp.sum(kept, axis=1)


def shards(queries, probes, targets, passage_codes, codebook):
    axes = ("corpus", "query")
    devices = lax.axis_size("corpus") * lax.axis_size("query")
    query_rows = queries.shape[0]
    list_total = passage_codes.shape[0] * lax.axis_size("corpus")
    lists = list_total // devices
    capacity = min(query_rows, max(2, 2 * PROBES * query_rows // list_total))
    slots = devices * capacity
    slot_count = lists * slots
    entries = PROBES * query_rows

    flat = probes.T.reshape(entries)
    ids = jnp.arange(entries, dtype=jnp.int32)
    earlier = (flat[:, None] == flat[None, :]) & (ids[None, :] < ids[:, None])
    rank = jnp.sum(earlier.astype(jnp.int32), axis=1)
    placed = ((flat % lists) * devices + flat // lists) * capacity + rank
    slot_ids = jnp.arange(slot_count, dtype=jnp.int32)
    hit = slot_ids[:, None] == placed[None, :]

    inside = targets[None] // PASSAGES == jnp.arange(PROBES, dtype=jnp.int32)[:, None, None]
    spot = targets[None] % PASSAGES
    notes = jnp.concatenate(
        [jnp.where(inside, spot // 256 + 1, 0), jnp.where(inside, spot % 256, 0)], axis=2
    ).reshape(entries, 2 * TARGETS)
    notes = jnp.pad(notes, ((0, 0), (0, NOTES - 2 * TARGETS))).astype(jnp.bfloat16)
    wide = jnp.concatenate([jnp.concatenate([queries] * PROBES, axis=0), notes], axis=1)
    sending = jnp.dot(
        hit.astype(jnp.bfloat16), wide, preferred_element_type=jnp.float32
    ).astype(jnp.bfloat16)

    def swap(x, axis=1):
        return lax.all_to_all(x, axes, split_axis=axis, concat_axis=axis, tiled=True)

    rows = swap(sending.reshape(lists, devices, capacity, WIDE)).reshape(lists, slots, WIDE)

    offset = (lax.axis_index("query") * lists).astype(jnp.int32).reshape(1)
    rows_spec = pl.BlockSpec((1, slots, WIDE), lambda i, off: (i, 0, 0))
    codes_spec = pl.BlockSpec((1, SUBSPACES, PASSAGES), lambda i, off: (off[0] + i, 0, 0))
    cb_spec = pl.BlockSpec((CENTROIDS, D), lambda i, off: (0, 0))
    exp_spec = pl.BlockSpec((1, slots, PASSAGES), lambda i, off: (i, 0, 0))
    table = pltpu.VMEM((3, CHUNKS, COLS, CHUNK), jnp.bfloat16)
    params = pltpu.CompilerParams(vmem_limit_bytes=40 * 2**20)

    exps, stats = pl.pallas_call(
        score_kernel,
        out_shape=(
            jax.ShapeDtypeStruct((lists, slots, PASSAGES), jnp.float32),
            jax.ShapeDtypeStruct((lists, 8, slots), jnp.float32),
        ),
        grid_spec=pltpu.PrefetchScalarGridSpec(
            num_scalar_prefetch=1,
            grid=(lists,),
            in_specs=[rows_spec, codes_spec, cb_spec],
            out_specs=(exp_spec, pl.BlockSpec((1, 8, slots), lambda i, off: (i, 0, 0))),
            scratch_shapes=[table],
        ),
        compiler_params=params,
        name="scores",
    )(offset, rows, passage_codes, codebook)

    back = swap(stats[:, :2].reshape(lists, 2, devices, capacity), 2)
    back_top = back[:, 0].reshape(slot_count)
    back_total = back[:, 1].reshape(slot_count)
    top = jnp.sum(jnp.where(hit, back_top[:, None], 0.0), axis=0).reshape(PROBES, query_rows)
    total = jnp.sum(jnp.where(hit, back_total[:, None], 0.0), axis=0).reshape(PROBES, query_rows)
    shrink = jnp.exp(top - jnp.max(top, axis=0))
    scale = (shrink / jnp.sum(total * shrink, axis=0)).reshape(entries)
    slot_scale = jnp.sum(jnp.where(hit, scale[None, :], 0.0), axis=1)
    factor = swap(slot_scale.reshape(lists, devices, capacity)).reshape(lists, 1, slots)

    part, raw = pl.pallas_call(
        grad_kernel,
        out_shape=(
            jax.ShapeDtypeStruct((lists, slots, D), jnp.bfloat16),
            jax.ShapeDtypeStruct((CENTROIDS, D), jnp.float32),
        ),
        grid_spec=pltpu.PrefetchScalarGridSpec(
            num_scalar_prefetch=1,
            grid=(lists,),
            in_specs=[
                rows_spec,
                codes_spec,
                cb_spec,
                exp_spec,
                pl.BlockSpec((1, 1, slots), lambda i, off: (i, 0, 0)),
            ],
            out_specs=(
                pl.BlockSpec((1, slots, D), lambda i, off: (i, 0, 0)),
                pl.BlockSpec((CENTROIDS, D), lambda i, off: (0, 0)),
            ),
            scratch_shapes=[table, pltpu.VMEM((CHUNKS, COLS, CHUNK), jnp.float32)],
        ),
        compiler_params=params,
        name="grads",
    )(offset, rows, passage_codes, codebook, exps, factor)

    raw = lax.psum(raw, axes)
    step = raw * lax.rsqrt(jnp.mean(raw * raw) + EPSILON)
    returned = swap(part.reshape(lists, devices, capacity, D)).reshape(slot_count, D)
    by_query = functools.reduce(
        jnp.logical_or,
        [
            slot_ids[None, :] == placed[p * query_rows : (p + 1) * query_rows, None]
            for p in range(PROBES)
        ],
    )
    grad = jnp.dot(by_query.astype(jnp.bfloat16), returned, preferred_element_type=jnp.float32)
    return (grad.astype(jnp.bfloat16), step)


def solution(mesh):
    placed = (
        P(("corpus", "query"), None),
        P(("corpus", "query"), None),
        P(("corpus", "query"), None),
        P("corpus", None, None),
        P(),
    )
    return jax.shard_map(
        shards,
        mesh=mesh,
        in_specs=placed,
        out_specs=(P(("corpus", "query"), None), P()),
        check_vma=False,
    )
```

```python
import functools

import jax
import jax.numpy as jnp
from jax import lax
from jax.experimental import pallas as pl
from jax.experimental.pallas import tpu as pltpu
from jax.sharding import PartitionSpec as P

D = 768
SUBSPACES = 96
CENTROIDS = 16
SUBDIM = 8
PASSAGES = 1024
PROBES = 4
TARGETS = 8
EPSILON = 1e-06

CHUNK = 128
CHUNKS = D // CHUNK
SPACES = CHUNK // SUBDIM
COLS = SPACES * CENTROIDS
PIECES = 2

NT = (((1,), (1,)), ((), ()))
TN = (((0,), (0,)), ((), ()))


def dot(a, b, dims=(((1,), (0,)), ((), ()))):
    return lax.dot_general(a, b, dims, preferred_element_type=jnp.float32)


def split(x, parts):
    out = []
    for _ in range(parts):
        top = x.astype(jnp.bfloat16)
        out.append(top)
        x = x - top.astype(jnp.float32)
    return out


def diagonal(shape):
    row = lax.broadcasted_iota(jnp.int32, shape, 1)
    col = lax.broadcasted_iota(jnp.int32, shape, 2)
    return row == col // SUBDIM


def fill_table(cb_ref, table):
    for c in range(CHUNKS):
        cb = cb_ref[:, c * CHUNK : (c + 1) * CHUNK]
        spread = jnp.broadcast_to(cb[:, None, :], (CENTROIDS, SPACES, CHUNK))
        spread = jnp.where(diagonal(spread.shape), spread, 0.0).reshape(COLS, CHUNK)
        for i, part in enumerate(split(spread, 3)):
            table[i, c] = part


def one_hot(codes_ref, c):
    codes = codes_ref[0, c * SPACES : (c + 1) * SPACES, :]
    return jnp.concatenate(
        [jnp.where(codes == k, 1.0, 0.0).astype(jnp.bfloat16) for k in range(CENTROIDS)], axis=0
    )


def score_kernel(off_ref, rows_ref, codes_ref, cb_ref, exp_ref, stat_ref, table):
    @pl.when(pl.program_id(0) == 0)
    def _():
        fill_table(cb_ref, table)

    scores = None
    for c in range(CHUNKS):
        row = rows_ref[0, :, c * CHUNK : (c + 1) * CHUNK]
        lut = dot(row, table[2, c], NT) + dot(row, table[1, c], NT) + dot(row, table[0, c], NT)
        term = dot(lut.astype(jnp.bfloat16), one_hot(codes_ref, c))
        scores = term if scores is None else scores + term
    top = jnp.max(scores, axis=1, keepdims=True)
    e = jnp.exp(scores - top)
    exp_ref[0] = e
    total = jnp.sum(e, axis=1, keepdims=True)
    lane = lax.broadcasted_iota(jnp.int32, (e.shape[0], 128), 1)
    stat_ref[0] = jnp.where(lane == 0, top, total).T[:8]


def grad_kernel(
    off_ref, rows_ref, codes_ref, cb_ref, exp_ref, factor_ref, part_ref, raw_ref, table, raw
):
    step = pl.program_id(0)

    @pl.when(step == 0)
    def _():
        fill_table(cb_ref, table)
        raw[...] = jnp.zeros_like(raw)

    slots = exp_ref.shape[1]
    held = factor_ref[0]
    held = jnp.concatenate([held, jnp.zeros((128 - held.shape[0], slots), jnp.float32)], axis=0).T
    factor = held[:, 0:1]
    spots = held.astype(jnp.int32) - 1
    place = lax.broadcasted_iota(jnp.int32, (slots, PASSAGES), 1)
    teacher = jnp.zeros((slots, PASSAGES), jnp.float32)
    for r in range(TARGETS):
        weight = 2.0 * (TARGETS - r) / (TARGETS * (TARGETS + 1.0))
        teacher = jnp.where(place == spots[:, r + 1 : r + 2], weight, teacher)
    grad = (exp_ref[0] * factor - teacher).astype(jnp.bfloat16)
    for c in range(CHUNKS):
        hist = dot(grad, one_hot(codes_ref, c), NT)
        hi, lo = split(hist, 2)
        part = dot(hi, table[0, c]) + dot(hi, table[1, c]) + dot(lo, table[0, c])
        part_ref[0, :, c * CHUNK : (c + 1) * CHUNK] = part.astype(jnp.bfloat16)
        row = rows_ref[0, :, c * CHUNK : (c + 1) * CHUNK]
        raw[c] += dot(hi, row, TN) + dot(lo, row, TN)

    @pl.when(step == pl.num_programs(0) - 1)
    def _():
        for c in range(CHUNKS):
            grid = raw[c].reshape(CENTROIDS, SPACES, CHUNK)
            kept = jnp.where(diagonal(grid.shape), grid, 0.0)
            raw_ref[:, c * CHUNK : (c + 1) * CHUNK] = jnp.sum(kept, axis=1)


def shards(queries, probes, targets, passage_codes, codebook):
    axes = ("corpus", "query")
    devices = lax.axis_size("corpus") * lax.axis_size("query")
    query_rows = queries.shape[0]
    list_total = passage_codes.shape[0] * lax.axis_size("corpus")
    lists = list_total // devices
    capacity = min(query_rows, max(2, 2 * PROBES * query_rows // list_total))
    slots = devices * capacity
    slot_count = lists * slots
    entries = PROBES * query_rows

    flat = probes.T.reshape(entries)
    ids = jnp.arange(entries, dtype=jnp.int32)
    earlier = (flat[:, None] == flat[None, :]) & (ids[None, :] < ids[:, None])
    rank = jnp.sum(earlier.astype(jnp.int32), axis=1)
    placed = ((flat % lists) * devices + flat // lists) * capacity + rank
    slot_ids = jnp.arange(slot_count, dtype=jnp.int32)
    hit = slot_ids[:, None] == placed[None, :]

    inside = targets[None] // PASSAGES == jnp.arange(PROBES, dtype=jnp.int32)[:, None, None]
    spot = targets[None] % PASSAGES
    hot = hit.astype(jnp.bfloat16)
    notes = jnp.concatenate(
        [jnp.where(inside, spot // 256, 0), jnp.where(inside, spot % 256, 0), inside], axis=2
    ).reshape(entries, 3 * TARGETS)
    notes = lax.dot_general(
        notes.astype(jnp.bfloat16), hot, (((0,), (1,)), ((), ())),
        preferred_element_type=jnp.float32,
    ).reshape(3, TARGETS, slot_count)
    notes = notes[0] * 256.0 + notes[1] + notes[2]

    def swap(x, axis=1):
        return lax.all_to_all(x, axes, split_axis=axis, concat_axis=axis, tiled=True)

    piece = lists // PIECES
    copies = jnp.concatenate([queries] * PROBES, axis=0)
    rows = []
    for i in range(PIECES):
        sending = jnp.dot(
            hot[i * piece * slots : (i + 1) * piece * slots],
            copies,
            preferred_element_type=jnp.float32,
        ).astype(jnp.bfloat16)
        rows.append(
            swap(sending.reshape(piece, devices, capacity, D)).reshape(piece, slots, D)
        )

    offsets = [
        (lax.axis_index("query") * lists + i * piece).astype(jnp.int32).reshape(1)
        for i in range(PIECES)
    ]
    work = 2 * piece * slots * COLS * CHUNKS * PASSAGES
    rows_spec = pl.BlockSpec((1, slots, D), lambda i, off: (i, 0, 0))
    codes_spec = pl.BlockSpec((1, SUBSPACES, PASSAGES), lambda i, off: (off[0] + i, 0, 0))
    cb_spec = pl.BlockSpec((CENTROIDS, D), lambda i, off: (0, 0))
    exp_spec = pl.BlockSpec((1, slots, PASSAGES), lambda i, off: (i, 0, 0))
    table = pltpu.VMEM((3, CHUNKS, COLS, CHUNK), jnp.bfloat16)
    params = pltpu.CompilerParams(vmem_limit_bytes=40 * 2**20)

    scored = pl.pallas_call(
        score_kernel,
        out_shape=(
            jax.ShapeDtypeStruct((piece, slots, PASSAGES), jnp.float32),
            jax.ShapeDtypeStruct((piece, 8, slots), jnp.float32),
        ),
        grid_spec=pltpu.PrefetchScalarGridSpec(
            num_scalar_prefetch=1,
            grid=(piece,),
            in_specs=[rows_spec, codes_spec, cb_spec],
            out_specs=(exp_spec, pl.BlockSpec((1, 8, slots), lambda i, off: (i, 0, 0))),
            scratch_shapes=[table],
        ),
        compiler_params=params,
        cost_estimate=pl.CostEstimate(
            flops=2 * work, bytes_accessed=8 * piece * slots * PASSAGES, transcendentals=0
        ),
        name="scores",
    )
    done = [scored(offsets[i], rows[i], passage_codes, codebook) for i in range(PIECES)]
    stats = jnp.concatenate([stat[:, :2] for _, stat in done], axis=0)

    back = swap(stats.reshape(lists, 2, devices, capacity), 2)
    back_top = back[:, 0].reshape(slot_count)
    back_total = back[:, 1].reshape(slot_count)
    top = jnp.sum(jnp.where(hit, back_top[:, None], 0.0), axis=0).reshape(PROBES, query_rows)
    total = jnp.sum(jnp.where(hit, back_total[:, None], 0.0), axis=0).reshape(PROBES, query_rows)
    shrink = jnp.exp(top - jnp.max(top, axis=0))
    scale = (shrink / jnp.sum(total * shrink, axis=0)).reshape(entries)
    slot_scale = jnp.sum(jnp.where(hit, scale[None, :], 0.0), axis=1)
    told = jnp.concatenate([slot_scale[None], notes], axis=0)
    told = told.reshape(TARGETS + 1, lists, devices, capacity).transpose(1, 0, 2, 3)
    told = swap(told, 2).reshape(lists, TARGETS + 1, slots)
    told = jnp.pad(told, ((0, 0), (0, 7), (0, 0)))

    graded = pl.pallas_call(
        grad_kernel,
        out_shape=(
            jax.ShapeDtypeStruct((piece, slots, D), jnp.bfloat16),
            jax.ShapeDtypeStruct((CENTROIDS, D), jnp.float32),
        ),
        grid_spec=pltpu.PrefetchScalarGridSpec(
            num_scalar_prefetch=1,
            grid=(piece,),
            in_specs=[
                rows_spec,
                codes_spec,
                cb_spec,
                exp_spec,
                pl.BlockSpec((1, TARGETS + 8, slots), lambda i, off: (i, 0, 0)),
            ],
            out_specs=(
                pl.BlockSpec((1, slots, D), lambda i, off: (i, 0, 0)),
                pl.BlockSpec((CENTROIDS, D), lambda i, off: (0, 0)),
            ),
            scratch_shapes=[table, pltpu.VMEM((CHUNKS, COLS, CHUNK), jnp.float32)],
        ),
        compiler_params=params,
        cost_estimate=pl.CostEstimate(
            flops=4 * work, bytes_accessed=8 * piece * slots * PASSAGES, transcendentals=0
        ),
        name="grads",
    )
    returned, raw = [], 0.0
    for i in range(PIECES):
        part, raw_part = graded(
            offsets[i],
            rows[i],
            passage_codes,
            codebook,
            done[i][0],
            told[i * piece : (i + 1) * piece],
        )
        raw = raw + raw_part
        part = swap(part.reshape(piece, devices, capacity, D))
        returned.append(part.reshape(piece * slots, D))

    raw = lax.psum(raw, axes)
    step = raw * lax.rsqrt(jnp.mean(raw * raw) + EPSILON)
    returned = jnp.concatenate(returned, axis=0)
    by_query = functools.reduce(
        jnp.logical_or,
        [
            slot_ids[None, :] == placed[p * query_rows : (p + 1) * query_rows, None]
            for p in range(PROBES)
        ],
    )
    grad = jnp.dot(by_query.astype(jnp.bfloat16), returned, preferred_element_type=jnp.float32)
    return (grad.astype(jnp.bfloat16), step)


def solution(mesh):
    placed = (
        P(("corpus", "query"), None),
        P(("corpus", "query"), None),
        P(("corpus", "query"), None),
        P("corpus", None, None),
        P(),
    )
    return jax.shard_map(
        shards,
        mesh=mesh,
        in_specs=placed,
        out_specs=(P(("corpus", "query"), None), P()),
        check_vma=False,
    )
```

```python
import functools

import jax
import jax.numpy as jnp
from jax import lax
from jax.experimental import pallas as pl
from jax.experimental.pallas import tpu as pltpu
from jax.sharding import PartitionSpec as P

D = 768
SUBSPACES = 96
CENTROIDS = 16
SUBDIM = 8
PASSAGES = 1024
PROBES = 4
TARGETS = 8
EPSILON = 1e-06

CHUNK = 128
CHUNKS = D // CHUNK
SPACES = CHUNK // SUBDIM
COLS = SPACES * CENTROIDS
PIECES = 2

NT = (((1,), (1,)), ((), ()))
TN = (((0,), (0,)), ((), ()))


def dot(a, b, dims=(((1,), (0,)), ((), ()))):
    return lax.dot_general(a, b, dims, preferred_element_type=jnp.float32)


def split(x, parts):
    out = []
    for _ in range(parts):
        top = x.astype(jnp.bfloat16)
        out.append(top)
        x = x - top.astype(jnp.float32)
    return out


def diagonal(shape):
    row = lax.broadcasted_iota(jnp.int32, shape, 1)
    col = lax.broadcasted_iota(jnp.int32, shape, 2)
    return row == col // SUBDIM


def fill_table(cb_ref, table):
    for c in range(CHUNKS):
        cb = cb_ref[:, c * CHUNK : (c + 1) * CHUNK]
        spread = jnp.broadcast_to(cb[:, None, :], (CENTROIDS, SPACES, CHUNK))
        spread = jnp.where(diagonal(spread.shape), spread, 0.0).reshape(COLS, CHUNK)
        for i, part in enumerate(split(spread, 3)):
            table[i, c] = part


def one_hot(codes_ref, c):
    codes = codes_ref[0, c * SPACES : (c + 1) * SPACES, :]
    return jnp.concatenate(
        [jnp.where(codes == k, 1.0, 0.0).astype(jnp.bfloat16) for k in range(CENTROIDS)], axis=0
    )


def score_kernel(off_ref, rows_ref, codes_ref, cb_ref, exp_ref, stat_ref, table):
    @pl.when(pl.program_id(0) == 0)
    def _():
        fill_table(cb_ref, table)

    scores = None
    for c in range(CHUNKS):
        row = rows_ref[0, :, c * CHUNK : (c + 1) * CHUNK]
        lut = dot(row, table[2, c], NT) + dot(row, table[1, c], NT) + dot(row, table[0, c], NT)
        term = dot(lut.astype(jnp.bfloat16), one_hot(codes_ref, c))
        scores = term if scores is None else scores + term
    top = jnp.max(scores, axis=1, keepdims=True)
    e = jnp.exp(scores - top)
    exp_ref[0] = e
    total = jnp.sum(e, axis=1, keepdims=True)
    lane = lax.broadcasted_iota(jnp.int32, (e.shape[0], 128), 1)
    stat_ref[0] = jnp.where(lane == 0, top, total).T[:8]


def grad_kernel(
    off_ref, rows_ref, codes_ref, cb_ref, exp_ref, factor_ref, notes_ref, part_ref, raw_ref, table, raw
):
    step = pl.program_id(0)

    @pl.when(step == 0)
    def _():
        fill_table(cb_ref, table)
        raw[...] = jnp.zeros_like(raw)

    slots = exp_ref.shape[1]
    factor = jnp.broadcast_to(factor_ref[0], (128, slots)).T[:, 0:1]
    notes = notes_ref[0]
    notes = jnp.concatenate([notes, jnp.zeros((128 - TARGETS, slots), jnp.float32)], axis=0).T
    spots = notes.astype(jnp.int32) - 1
    place = lax.broadcasted_iota(jnp.int32, (slots, PASSAGES), 1)
    teacher = jnp.zeros((slots, PASSAGES), jnp.float32)
    for r in range(TARGETS):
        weight = 2.0 * (TARGETS - r) / (TARGETS * (TARGETS + 1.0))
        teacher = jnp.where(place == spots[:, r : r + 1], weight, teacher)
    grad = (exp_ref[0] * factor - teacher).astype(jnp.bfloat16)
    for c in range(CHUNKS):
        hist = dot(grad, one_hot(codes_ref, c), NT)
        hi, lo = split(hist, 2)
        part = dot(hi, table[0, c]) + dot(hi, table[1, c]) + dot(lo, table[0, c])
        part_ref[0, :, c * CHUNK : (c + 1) * CHUNK] = part.astype(jnp.bfloat16)
        row = rows_ref[0, :, c * CHUNK : (c + 1) * CHUNK]
        raw[c] += dot(hi, row, TN) + dot(lo, row, TN)

    @pl.when(step == pl.num_programs(0) - 1)
    def _():
        for c in range(CHUNKS):
            grid = raw[c].reshape(CENTROIDS, SPACES, CHUNK)
            kept = jnp.where(diagonal(grid.shape), grid, 0.0)
            raw_ref[:, c * CHUNK : (c + 1) * CHUNK] = jnp.sum(kept, axis=1)


def shards(queries, probes, targets, passage_codes, codebook):
    axes = ("corpus", "query")
    devices = lax.axis_size("corpus") * lax.axis_size("query")
    query_rows = queries.shape[0]
    list_total = passage_codes.shape[0] * lax.axis_size("corpus")
    lists = list_total // devices
    capacity = min(query_rows, max(2, 2 * PROBES * query_rows // list_total))
    slots = devices * capacity
    slot_count = lists * slots
    entries = PROBES * query_rows

    flat = probes.T.reshape(entries)
    ids = jnp.arange(entries, dtype=jnp.int32)
    earlier = (flat[:, None] == flat[None, :]) & (ids[None, :] < ids[:, None])
    rank = jnp.sum(earlier.astype(jnp.int32), axis=1)
    placed = ((flat % lists) * devices + flat // lists) * capacity + rank
    slot_ids = jnp.arange(slot_count, dtype=jnp.int32)
    hit = slot_ids[:, None] == placed[None, :]

    inside = targets[None] // PASSAGES == jnp.arange(PROBES, dtype=jnp.int32)[:, None, None]
    spot = targets[None] % PASSAGES
    hot = hit.astype(jnp.bfloat16)
    notes = jnp.concatenate(
        [jnp.where(inside, spot // 256, 0), jnp.where(inside, spot % 256, 0), inside], axis=2
    ).reshape(entries, 3 * TARGETS)
    notes = lax.dot_general(
        notes.astype(jnp.bfloat16), hot, (((0,), (1,)), ((), ())),
        preferred_element_type=jnp.float32,
    ).reshape(3, TARGETS, slot_count)
    notes = notes[0] * 256.0 + notes[1] + notes[2]

    def swap(x, axis=1):
        return lax.all_to_all(x, axes, split_axis=axis, concat_axis=axis, tiled=True)

    piece = lists // PIECES
    copies = jnp.concatenate([queries] * PROBES, axis=0)
    rows = []
    for i in range(PIECES):
        sending = jnp.dot(
            hot[i * piece * slots : (i + 1) * piece * slots],
            copies,
            preferred_element_type=jnp.float32,
        ).astype(jnp.bfloat16)
        rows.append(
            swap(sending.reshape(piece, devices, capacity, D)).reshape(piece, slots, D)
        )

    notes = swap(notes.reshape(TARGETS, lists, devices, capacity), 2)
    notes = notes.reshape(TARGETS, lists, slots).transpose(1, 0, 2)

    offsets = [
        (lax.axis_index("query") * lists + i * piece).astype(jnp.int32).reshape(1)
        for i in range(PIECES)
    ]
    work = 2 * piece * slots * COLS * CHUNKS * PASSAGES
    rows_spec = pl.BlockSpec((1, slots, D), lambda i, off: (i, 0, 0))
    codes_spec = pl.BlockSpec((1, SUBSPACES, PASSAGES), lambda i, off: (off[0] + i, 0, 0))
    cb_spec = pl.BlockSpec((CENTROIDS, D), lambda i, off: (0, 0))
    exp_spec = pl.BlockSpec((1, slots, PASSAGES), lambda i, off: (i, 0, 0))
    table = pltpu.VMEM((3, CHUNKS, COLS, CHUNK), jnp.bfloat16)
    params = pltpu.CompilerParams(vmem_limit_bytes=40 * 2**20)

    scored = pl.pallas_call(
        score_kernel,
        out_shape=(
            jax.ShapeDtypeStruct((piece, slots, PASSAGES), jnp.float32),
            jax.ShapeDtypeStruct((piece, 8, slots), jnp.float32),
        ),
        grid_spec=pltpu.PrefetchScalarGridSpec(
            num_scalar_prefetch=1,
            grid=(piece,),
            in_specs=[rows_spec, codes_spec, cb_spec],
            out_specs=(exp_spec, pl.BlockSpec((1, 8, slots), lambda i, off: (i, 0, 0))),
            scratch_shapes=[table],
        ),
        compiler_params=params,
        cost_estimate=pl.CostEstimate(
            flops=2 * work, bytes_accessed=8 * piece * slots * PASSAGES, transcendentals=0
        ),
        name="scores",
    )
    done = [scored(offsets[i], rows[i], passage_codes, codebook) for i in range(PIECES)]
    stats = jnp.concatenate([stat[:, :2] for _, stat in done], axis=0)

    back = swap(stats.reshape(lists, 2, devices, capacity), 2)
    back_top = back[:, 0].reshape(slot_count)
    back_total = back[:, 1].reshape(slot_count)
    top = jnp.sum(jnp.where(hit, back_top[:, None], 0.0), axis=0).reshape(PROBES, query_rows)
    total = jnp.sum(jnp.where(hit, back_total[:, None], 0.0), axis=0).reshape(PROBES, query_rows)
    shrink = jnp.exp(top - jnp.max(top, axis=0))
    scale = (shrink / jnp.sum(total * shrink, axis=0)).reshape(entries)
    slot_scale = jnp.sum(jnp.where(hit, scale[None, :], 0.0), axis=1)
    factor = swap(slot_scale.reshape(lists, devices, capacity)).reshape(lists, 1, slots)

    graded = pl.pallas_call(
        grad_kernel,
        out_shape=(
            jax.ShapeDtypeStruct((piece, slots, D), jnp.bfloat16),
            jax.ShapeDtypeStruct((CENTROIDS, D), jnp.float32),
        ),
        grid_spec=pltpu.PrefetchScalarGridSpec(
            num_scalar_prefetch=1,
            grid=(piece,),
            in_specs=[
                rows_spec,
                codes_spec,
                cb_spec,
                exp_spec,
                pl.BlockSpec((1, 1, slots), lambda i, off: (i, 0, 0)),
                pl.BlockSpec((1, TARGETS, slots), lambda i, off: (i, 0, 0)),
            ],
            out_specs=(
                pl.BlockSpec((1, slots, D), lambda i, off: (i, 0, 0)),
                pl.BlockSpec((CENTROIDS, D), lambda i, off: (0, 0)),
            ),
            scratch_shapes=[table, pltpu.VMEM((CHUNKS, COLS, CHUNK), jnp.float32)],
        ),
        compiler_params=params,
        cost_estimate=pl.CostEstimate(
            flops=4 * work, bytes_accessed=8 * piece * slots * PASSAGES, transcendentals=0
        ),
        name="grads",
    )
    returned, raw = [], 0.0
    for i in range(PIECES):
        part, raw_part = graded(
            offsets[i],
            rows[i],
            passage_codes,
            codebook,
            done[i][0],
            factor[i * piece : (i + 1) * piece],
            notes[i * piece : (i + 1) * piece],
        )
        raw = raw + raw_part
        part = swap(part.reshape(piece, devices, capacity, D))
        returned.append(part.reshape(piece * slots, D))

    raw = lax.psum(raw, axes)
    step = raw * lax.rsqrt(jnp.mean(raw * raw) + EPSILON)
    returned = jnp.concatenate(returned, axis=0)
    by_query = functools.reduce(
        jnp.logical_or,
        [
            slot_ids[None, :] == placed[p * query_rows : (p + 1) * query_rows, None]
            for p in range(PROBES)
        ],
    )
    grad = jnp.dot(by_query.astype(jnp.bfloat16), returned, preferred_element_type=jnp.float32)
    return (grad.astype(jnp.bfloat16), step)


def solution(mesh):
    placed = (
        P(("corpus", "query"), None),
        P(("corpus", "query"), None),
        P(("corpus", "query"), None),
        P("corpus", None, None),
        P(),
    )
    return jax.shard_map(
        shards,
        mesh=mesh,
        in_specs=placed,
        out_specs=(P(("corpus", "query"), None), P()),
        check_vma=False,
    )
```

```python
import functools

import jax
import jax.numpy as jnp
from jax import lax
from jax.experimental import pallas as pl
from jax.experimental.pallas import tpu as pltpu
from jax.sharding import PartitionSpec as P

D = 768
SUBSPACES = 96
CENTROIDS = 16
SUBDIM = 8
PASSAGES = 1024
PROBES = 4
TARGETS = 8
EPSILON = 1e-06

CHUNK = 128
CHUNKS = D // CHUNK
SPACES = CHUNK // SUBDIM
COLS = SPACES * CENTROIDS
PIECES = 2

NT = (((1,), (1,)), ((), ()))
TN = (((0,), (0,)), ((), ()))


def dot(a, b, dims=(((1,), (0,)), ((), ()))):
    return lax.dot_general(a, b, dims, preferred_element_type=jnp.float32)


def split(x, parts):
    out = []
    for _ in range(parts):
        top = x.astype(jnp.bfloat16)
        out.append(top)
        x = x - top.astype(jnp.float32)
    return out


def diagonal(shape):
    row = lax.broadcasted_iota(jnp.int32, shape, 1)
    col = lax.broadcasted_iota(jnp.int32, shape, 2)
    return row == col // SUBDIM


def fill_table(cb_ref, table):
    for c in range(CHUNKS):
        cb = cb_ref[:, c * CHUNK : (c + 1) * CHUNK]
        spread = jnp.broadcast_to(cb[:, None, :], (CENTROIDS, SPACES, CHUNK))
        spread = jnp.where(diagonal(spread.shape), spread, 0.0).reshape(COLS, CHUNK)
        for i, part in enumerate(split(spread, 3)):
            table[i, c] = part


def one_hot(codes_ref, c):
    codes = codes_ref[0, c * SPACES : (c + 1) * SPACES, :]
    return jnp.concatenate(
        [jnp.where(codes == k, 1.0, 0.0).astype(jnp.bfloat16) for k in range(CENTROIDS)], axis=0
    )


def score_kernel(off_ref, rows_ref, codes_ref, cb_ref, exp_ref, stat_ref, table):
    @pl.when(pl.program_id(0) == 0)
    def _():
        fill_table(cb_ref, table)

    scores = None
    for c in range(CHUNKS):
        row = rows_ref[0, :, c * CHUNK : (c + 1) * CHUNK]
        lut = dot(row, table[2, c], NT) + dot(row, table[1, c], NT) + dot(row, table[0, c], NT)
        term = dot(lut.astype(jnp.bfloat16), one_hot(codes_ref, c))
        scores = term if scores is None else scores + term
    top = jnp.max(scores, axis=1, keepdims=True)
    e = jnp.exp(scores - top)
    exp_ref[0] = e
    total = jnp.sum(e, axis=1, keepdims=True)
    lane = lax.broadcasted_iota(jnp.int32, (e.shape[0], 128), 1)
    stat_ref[0] = jnp.where(lane == 0, top, total).T[:8]


def grad_kernel(
    off_ref, rows_ref, codes_ref, cb_ref, exp_ref, factor_ref, notes_ref, part_ref, raw_ref, table, raw
):
    step = pl.program_id(0)

    @pl.when(step == 0)
    def _():
        fill_table(cb_ref, table)
        raw[...] = jnp.zeros_like(raw)

    slots = exp_ref.shape[1]
    factor = jnp.broadcast_to(factor_ref[0], (128, slots)).T[:, 0:1]
    notes = notes_ref[0]
    notes = jnp.concatenate([notes, jnp.zeros((128 - TARGETS, slots), jnp.float32)], axis=0).T
    spots = notes.astype(jnp.int32) - 1
    place = lax.broadcasted_iota(jnp.int32, (slots, PASSAGES), 1)
    teacher = jnp.zeros((slots, PASSAGES), jnp.float32)
    for r in range(TARGETS):
        weight = 2.0 * (TARGETS - r) / (TARGETS * (TARGETS + 1.0))
        teacher = jnp.where(place == spots[:, r : r + 1], weight, teacher)
    grad = (exp_ref[0] * factor - teacher).astype(jnp.bfloat16)
    for c in range(CHUNKS):
        hist = dot(grad, one_hot(codes_ref, c), NT)
        hi, lo = split(hist, 2)
        part = dot(hi, table[0, c]) + dot(hi, table[1, c]) + dot(lo, table[0, c])
        part_ref[0, :, c * CHUNK : (c + 1) * CHUNK] = part.astype(jnp.bfloat16)
        row = rows_ref[0, :, c * CHUNK : (c + 1) * CHUNK]
        raw[c] += dot(hi, row, TN) + dot(lo, row, TN)

    @pl.when(step == pl.num_programs(0) - 1)
    def _():
        for c in range(CHUNKS):
            grid = raw[c].reshape(CENTROIDS, SPACES, CHUNK)
            kept = jnp.where(diagonal(grid.shape), grid, 0.0)
            raw_ref[:, c * CHUNK : (c + 1) * CHUNK] = jnp.sum(kept, axis=1)


def shards(queries, probes, targets, passage_codes, codebook):
    axes = ("corpus", "query")
    devices = lax.axis_size("corpus") * lax.axis_size("query")
    query_rows = queries.shape[0]
    list_total = passage_codes.shape[0] * lax.axis_size("corpus")
    lists = list_total // devices
    capacity = min(query_rows, max(2, 2 * PROBES * query_rows // list_total))
    slots = devices * capacity
    slot_count = lists * slots
    entries = PROBES * query_rows

    flat = probes.T.reshape(entries)
    ids = jnp.arange(entries, dtype=jnp.int32)
    earlier = (flat[:, None] == flat[None, :]) & (ids[None, :] < ids[:, None])
    rank = jnp.sum(earlier.astype(jnp.int32), axis=1)
    placed = ((flat % lists) * devices + flat // lists) * capacity + rank
    slot_ids = jnp.arange(slot_count, dtype=jnp.int32)
    hit = slot_ids[:, None] == placed[None, :]

    inside = targets[None] // PASSAGES == jnp.arange(PROBES, dtype=jnp.int32)[:, None, None]
    spot = targets[None] % PASSAGES
    hot = hit.astype(jnp.bfloat16)
    notes = jnp.concatenate(
        [jnp.where(inside, spot // 256, 0), jnp.where(inside, spot % 256, 0), inside], axis=2
    ).reshape(entries, 3 * TARGETS)
    notes = lax.dot_general(
        notes.astype(jnp.bfloat16), hot, (((0,), (1,)), ((), ())),
        preferred_element_type=jnp.float32,
    ).reshape(3, TARGETS, slot_count)
    notes = notes[0] * 256.0 + notes[1] + notes[2]

    def swap(x, axis=1):
        return lax.all_to_all(x, axes, split_axis=axis, concat_axis=axis, tiled=True)

    piece = lists // PIECES
    copies = jnp.concatenate([queries] * PROBES, axis=0)
    rows = []
    for i in range(PIECES):
        sending = jnp.dot(
            hot[i * piece * slots : (i + 1) * piece * slots],
            copies,
            preferred_element_type=jnp.float32,
        ).astype(jnp.bfloat16)
        rows.append(
            swap(sending.reshape(piece, devices, capacity, D)).reshape(piece, slots, D)
        )

    notes = swap(notes.reshape(TARGETS, lists, devices, capacity), 2)
    notes = notes.reshape(TARGETS, lists, slots).transpose(1, 0, 2)

    offsets = [
        (lax.axis_index("query") * lists + i * piece).astype(jnp.int32).reshape(1)
        for i in range(PIECES)
    ]
    work = 2 * piece * slots * COLS * CHUNKS * PASSAGES
    rows_spec = pl.BlockSpec((1, slots, D), lambda i, off: (i, 0, 0))
    codes_spec = pl.BlockSpec((1, SUBSPACES, PASSAGES), lambda i, off: (off[0] + i, 0, 0))
    cb_spec = pl.BlockSpec((CENTROIDS, D), lambda i, off: (0, 0))
    exp_spec = pl.BlockSpec((1, slots, PASSAGES), lambda i, off: (i, 0, 0))
    table = pltpu.VMEM((3, CHUNKS, COLS, CHUNK), jnp.bfloat16)
    params = pltpu.CompilerParams(vmem_limit_bytes=40 * 2**20)

    scored = pl.pallas_call(
        score_kernel,
        out_shape=(
            jax.ShapeDtypeStruct((piece, slots, PASSAGES), jnp.float32),
            jax.ShapeDtypeStruct((piece, 8, slots), jnp.float32),
        ),
        grid_spec=pltpu.PrefetchScalarGridSpec(
            num_scalar_prefetch=1,
            grid=(piece,),
            in_specs=[rows_spec, codes_spec, cb_spec],
            out_specs=(exp_spec, pl.BlockSpec((1, 8, slots), lambda i, off: (i, 0, 0))),
            scratch_shapes=[table],
        ),
        compiler_params=params,
        cost_estimate=pl.CostEstimate(
            flops=2 * work, bytes_accessed=8 * piece * slots * PASSAGES, transcendentals=0
        ),
        name="scores",
    )
    done = [scored(offsets[i], rows[i], passage_codes, codebook) for i in range(PIECES)]
    stats = jnp.concatenate([stat[:, :2] for _, stat in done], axis=0)

    back = swap(stats.reshape(lists, 2, devices, capacity), 2)
    back_top = back[:, 0].reshape(slot_count)
    back_total = back[:, 1].reshape(slot_count)
    top = jnp.sum(jnp.where(hit, back_top[:, None], 0.0), axis=0).reshape(PROBES, query_rows)
    total = jnp.sum(jnp.where(hit, back_total[:, None], 0.0), axis=0).reshape(PROBES, query_rows)
    shrink = jnp.exp(top - jnp.max(top, axis=0))
    scale = (shrink / jnp.sum(total * shrink, axis=0)).reshape(entries)
    slot_scale = jnp.sum(jnp.where(hit, scale[None, :], 0.0), axis=1)
    factor = swap(slot_scale.reshape(lists, devices, capacity)).reshape(lists, 1, slots)

    graded = pl.pallas_call(
        grad_kernel,
        out_shape=(
            jax.ShapeDtypeStruct((piece, slots, D), jnp.bfloat16),
            jax.ShapeDtypeStruct((CENTROIDS, D), jnp.float32),
        ),
        grid_spec=pltpu.PrefetchScalarGridSpec(
            num_scalar_prefetch=1,
            grid=(piece,),
            in_specs=[
                rows_spec,
                codes_spec,
                cb_spec,
                exp_spec,
                pl.BlockSpec((1, 1, slots), lambda i, off: (i, 0, 0)),
                pl.BlockSpec((1, TARGETS, slots), lambda i, off: (i, 0, 0)),
            ],
            out_specs=(
                pl.BlockSpec((1, slots, D), lambda i, off: (i, 0, 0)),
                pl.BlockSpec((CENTROIDS, D), lambda i, off: (0, 0)),
            ),
            scratch_shapes=[table, pltpu.VMEM((CHUNKS, COLS, CHUNK), jnp.float32)],
        ),
        compiler_params=params,
        cost_estimate=pl.CostEstimate(
            flops=4 * work, bytes_accessed=8 * piece * slots * PASSAGES, transcendentals=0
        ),
        name="grads",
    )
    returned, raw = [], 0.0
    for i in range(PIECES):
        part, raw_part = graded(
            offsets[i],
            rows[i],
            passage_codes,
            codebook,
            done[i][0],
            factor[i * piece : (i + 1) * piece],
            notes[i * piece : (i + 1) * piece],
        )
        raw = raw + raw_part
        if i == PIECES - 1:
            part, raw = lax.optimization_barrier((part, lax.psum(raw, axes)))
        part = swap(part.reshape(piece, devices, capacity, D))
        returned.append(part.reshape(piece * slots, D))

    step = raw * lax.rsqrt(jnp.mean(raw * raw) + EPSILON)
    returned = jnp.concatenate(returned, axis=0)
    by_query = functools.reduce(
        jnp.logical_or,
        [
            slot_ids[None, :] == placed[p * query_rows : (p + 1) * query_rows, None]
            for p in range(PROBES)
        ],
    )
    grad = jnp.dot(by_query.astype(jnp.bfloat16), returned, preferred_element_type=jnp.float32)
    return (grad.astype(jnp.bfloat16), step)


def solution(mesh):
    placed = (
        P(("corpus", "query"), None),
        P(("corpus", "query"), None),
        P(("corpus", "query"), None),
        P("corpus", None, None),
        P(),
    )
    return jax.shard_map(
        shards,
        mesh=mesh,
        in_specs=placed,
        out_specs=(P(("corpus", "query"), None), P()),
        check_vma=False,
    )
```

```python
import functools

import jax
import jax.numpy as jnp
from jax import lax
from jax.experimental import pallas as pl
from jax.experimental.pallas import tpu as pltpu
from jax.sharding import PartitionSpec as P

D = 768
SUBSPACES = 96
CENTROIDS = 16
SUBDIM = 8
PASSAGES = 1024
PROBES = 4
TARGETS = 8
EPSILON = 1e-06

CHUNK = 128
CHUNKS = D // CHUNK
SPACES = CHUNK // SUBDIM
COLS = SPACES * CENTROIDS
PIECES = 4

NT = (((1,), (1,)), ((), ()))
TN = (((0,), (0,)), ((), ()))


def dot(a, b, dims=(((1,), (0,)), ((), ()))):
    return lax.dot_general(a, b, dims, preferred_element_type=jnp.float32)


def split(x, parts):
    out = []
    for _ in range(parts):
        top = x.astype(jnp.bfloat16)
        out.append(top)
        x = x - top.astype(jnp.float32)
    return out


def diagonal(shape):
    row = lax.broadcasted_iota(jnp.int32, shape, 1)
    col = lax.broadcasted_iota(jnp.int32, shape, 2)
    return row == col // SUBDIM


def fill_table(cb_ref, table):
    for c in range(CHUNKS):
        cb = cb_ref[:, c * CHUNK : (c + 1) * CHUNK]
        spread = jnp.broadcast_to(cb[:, None, :], (CENTROIDS, SPACES, CHUNK))
        spread = jnp.where(diagonal(spread.shape), spread, 0.0).reshape(COLS, CHUNK)
        for i, part in enumerate(split(spread, 3)):
            table[i, c] = part


def one_hot(codes_ref, c):
    codes = codes_ref[0, c * SPACES : (c + 1) * SPACES, :]
    return jnp.concatenate(
        [jnp.where(codes == k, 1.0, 0.0).astype(jnp.bfloat16) for k in range(CENTROIDS)], axis=0
    )


def score_kernel(off_ref, rows_ref, codes_ref, cb_ref, exp_ref, stat_ref, table):
    @pl.when(pl.program_id(0) == 0)
    def _():
        fill_table(cb_ref, table)

    scores = None
    for c in range(CHUNKS):
        row = rows_ref[0, :, c * CHUNK : (c + 1) * CHUNK]
        lut = dot(row, table[2, c], NT) + dot(row, table[1, c], NT) + dot(row, table[0, c], NT)
        term = dot(lut.astype(jnp.bfloat16), one_hot(codes_ref, c))
        scores = term if scores is None else scores + term
    top = jnp.max(scores, axis=1, keepdims=True)
    e = jnp.exp(scores - top)
    exp_ref[0] = e
    total = jnp.sum(e, axis=1, keepdims=True)
    lane = lax.broadcasted_iota(jnp.int32, (e.shape[0], 128), 1)
    stat_ref[0] = jnp.where(lane == 0, top, total).T[:8]


def grad_kernel(
    off_ref, rows_ref, codes_ref, cb_ref, exp_ref, factor_ref, notes_ref, part_ref, raw_ref, table, raw
):
    step = pl.program_id(0)

    @pl.when(step == 0)
    def _():
        fill_table(cb_ref, table)
        raw[...] = jnp.zeros_like(raw)

    slots = exp_ref.shape[1]
    factor = jnp.broadcast_to(factor_ref[0], (128, slots)).T[:, 0:1]
    notes = notes_ref[0]
    notes = jnp.concatenate([notes, jnp.zeros((128 - TARGETS, slots), jnp.float32)], axis=0).T
    spots = notes.astype(jnp.int32) - 1
    place = lax.broadcasted_iota(jnp.int32, (slots, PASSAGES), 1)
    teacher = jnp.zeros((slots, PASSAGES), jnp.float32)
    for r in range(TARGETS):
        weight = 2.0 * (TARGETS - r) / (TARGETS * (TARGETS + 1.0))
        teacher = jnp.where(place == spots[:, r : r + 1], weight, teacher)
    grad = (exp_ref[0] * factor - teacher).astype(jnp.bfloat16)
    for c in range(CHUNKS):
        hist = dot(grad, one_hot(codes_ref, c), NT)
        hi, lo = split(hist, 2)
        part = dot(hi, table[0, c]) + dot(hi, table[1, c]) + dot(lo, table[0, c])
        part_ref[0, :, c * CHUNK : (c + 1) * CHUNK] = part.astype(jnp.bfloat16)
        row = rows_ref[0, :, c * CHUNK : (c + 1) * CHUNK]
        raw[c] += dot(hi, row, TN) + dot(lo, row, TN)

    @pl.when(step == pl.num_programs(0) - 1)
    def _():
        for c in range(CHUNKS):
            grid = raw[c].reshape(CENTROIDS, SPACES, CHUNK)
            kept = jnp.where(diagonal(grid.shape), grid, 0.0)
            raw_ref[:, c * CHUNK : (c + 1) * CHUNK] = jnp.sum(kept, axis=1)


def shards(queries, probes, targets, passage_codes, codebook):
    axes = ("corpus", "query")
    devices = lax.axis_size("corpus") * lax.axis_size("query")
    query_rows = queries.shape[0]
    list_total = passage_codes.shape[0] * lax.axis_size("corpus")
    lists = list_total // devices
    capacity = min(query_rows, max(2, 2 * PROBES * query_rows // list_total))
    slots = devices * capacity
    slot_count = lists * slots
    entries = PROBES * query_rows

    flat = probes.T.reshape(entries)
    ids = jnp.arange(entries, dtype=jnp.int32)
    earlier = (flat[:, None] == flat[None, :]) & (ids[None, :] < ids[:, None])
    rank = jnp.sum(earlier.astype(jnp.int32), axis=1)
    placed = ((flat % lists) * devices + flat // lists) * capacity + rank
    slot_ids = jnp.arange(slot_count, dtype=jnp.int32)
    hit = slot_ids[:, None] == placed[None, :]

    inside = targets[None] // PASSAGES == jnp.arange(PROBES, dtype=jnp.int32)[:, None, None]
    spot = targets[None] % PASSAGES
    hot = hit.astype(jnp.bfloat16)
    notes = jnp.concatenate(
        [jnp.where(inside, spot // 256, 0), jnp.where(inside, spot % 256, 0), inside], axis=2
    ).reshape(entries, 3 * TARGETS)
    notes = lax.dot_general(
        notes.astype(jnp.bfloat16), hot, (((0,), (1,)), ((), ())),
        preferred_element_type=jnp.float32,
    ).reshape(3, TARGETS, slot_count)
    notes = notes[0] * 256.0 + notes[1] + notes[2]

    def swap(x, axis=1):
        return lax.all_to_all(x, axes, split_axis=axis, concat_axis=axis, tiled=True)

    piece = lists // PIECES
    copies = jnp.concatenate([queries] * PROBES, axis=0)
    rows = []
    for i in range(PIECES):
        sending = jnp.dot(
            hot[i * piece * slots : (i + 1) * piece * slots],
            copies,
            preferred_element_type=jnp.float32,
        ).astype(jnp.bfloat16)
        rows.append(
            swap(sending.reshape(piece, devices, capacity, D)).reshape(piece, slots, D)
        )

    notes = swap(notes.reshape(TARGETS, lists, devices, capacity), 2)
    notes = notes.reshape(TARGETS, lists, slots).transpose(1, 0, 2)

    offsets = [
        (lax.axis_index("query") * lists + i * piece).astype(jnp.int32).reshape(1)
        for i in range(PIECES)
    ]
    work = 2 * piece * slots * COLS * CHUNKS * PASSAGES
    rows_spec = pl.BlockSpec((1, slots, D), lambda i, off: (i, 0, 0))
    codes_spec = pl.BlockSpec((1, SUBSPACES, PASSAGES), lambda i, off: (off[0] + i, 0, 0))
    cb_spec = pl.BlockSpec((CENTROIDS, D), lambda i, off: (0, 0))
    exp_spec = pl.BlockSpec((1, slots, PASSAGES), lambda i, off: (i, 0, 0))
    table = pltpu.VMEM((3, CHUNKS, COLS, CHUNK), jnp.bfloat16)
    params = pltpu.CompilerParams(vmem_limit_bytes=40 * 2**20)

    scored = pl.pallas_call(
        score_kernel,
        out_shape=(
            jax.ShapeDtypeStruct((piece, slots, PASSAGES), jnp.float32),
            jax.ShapeDtypeStruct((piece, 8, slots), jnp.float32),
        ),
        grid_spec=pltpu.PrefetchScalarGridSpec(
            num_scalar_prefetch=1,
            grid=(piece,),
            in_specs=[rows_spec, codes_spec, cb_spec],
            out_specs=(exp_spec, pl.BlockSpec((1, 8, slots), lambda i, off: (i, 0, 0))),
            scratch_shapes=[table],
        ),
        compiler_params=params,
        cost_estimate=pl.CostEstimate(
            flops=2 * work, bytes_accessed=8 * piece * slots * PASSAGES, transcendentals=0
        ),
        name="scores",
    )
    done = [scored(offsets[i], rows[i], passage_codes, codebook) for i in range(PIECES)]
    stats = jnp.concatenate([stat[:, :2] for _, stat in done], axis=0)

    back = swap(stats.reshape(lists, 2, devices, capacity), 2)
    back_top = back[:, 0].reshape(slot_count)
    back_total = back[:, 1].reshape(slot_count)
    top = jnp.sum(jnp.where(hit, back_top[:, None], 0.0), axis=0).reshape(PROBES, query_rows)
    total = jnp.sum(jnp.where(hit, back_total[:, None], 0.0), axis=0).reshape(PROBES, query_rows)
    shrink = jnp.exp(top - jnp.max(top, axis=0))
    scale = (shrink / jnp.sum(total * shrink, axis=0)).reshape(entries)
    slot_scale = jnp.sum(jnp.where(hit, scale[None, :], 0.0), axis=1)
    factor = swap(slot_scale.reshape(lists, devices, capacity)).reshape(lists, 1, slots)

    graded = pl.pallas_call(
        grad_kernel,
        out_shape=(
            jax.ShapeDtypeStruct((piece, slots, D), jnp.bfloat16),
            jax.ShapeDtypeStruct((CENTROIDS, D), jnp.float32),
        ),
        grid_spec=pltpu.PrefetchScalarGridSpec(
            num_scalar_prefetch=1,
            grid=(piece,),
            in_specs=[
                rows_spec,
                codes_spec,
                cb_spec,
                exp_spec,
                pl.BlockSpec((1, 1, slots), lambda i, off: (i, 0, 0)),
                pl.BlockSpec((1, TARGETS, slots), lambda i, off: (i, 0, 0)),
            ],
            out_specs=(
                pl.BlockSpec((1, slots, D), lambda i, off: (i, 0, 0)),
                pl.BlockSpec((CENTROIDS, D), lambda i, off: (0, 0)),
            ),
            scratch_shapes=[table, pltpu.VMEM((CHUNKS, COLS, CHUNK), jnp.float32)],
        ),
        compiler_params=params,
        cost_estimate=pl.CostEstimate(
            flops=4 * work, bytes_accessed=8 * piece * slots * PASSAGES, transcendentals=0
        ),
        name="grads",
    )
    returned, raw = [], 0.0
    for i in range(PIECES):
        part, raw_part = graded(
            offsets[i],
            rows[i],
            passage_codes,
            codebook,
            done[i][0],
            factor[i * piece : (i + 1) * piece],
            notes[i * piece : (i + 1) * piece],
        )
        raw = raw + raw_part
        part = swap(part.reshape(piece, devices, capacity, D))
        returned.append(part.reshape(piece * slots, D))

    raw = lax.psum(raw, axes)
    step = raw * lax.rsqrt(jnp.mean(raw * raw) + EPSILON)
    returned = jnp.concatenate(returned, axis=0)
    by_query = functools.reduce(
        jnp.logical_or,
        [
            slot_ids[None, :] == placed[p * query_rows : (p + 1) * query_rows, None]
            for p in range(PROBES)
        ],
    )
    grad = jnp.dot(by_query.astype(jnp.bfloat16), returned, preferred_element_type=jnp.float32)
    return (grad.astype(jnp.bfloat16), step)


def solution(mesh):
    placed = (
        P(("corpus", "query"), None),
        P(("corpus", "query"), None),
        P(("corpus", "query"), None),
        P("corpus", None, None),
        P(),
    )
    return jax.shard_map(
        shards,
        mesh=mesh,
        in_specs=placed,
        out_specs=(P(("corpus", "query"), None), P()),
        check_vma=False,
    )
```
